768 devices in a mesh: dp: 24 (over z, core), seq: 32 (over y, x).
Axes of the slice: x: 4, y: 8, z: 12, core: 2. Of those that a mesh axis runs over, the one named last changes fastest.
Arguments:
- enc: bfloat16 [98304, 2048], P(('dp', 'seq')), may hold values from -6 to 6
- enc_dest: int32 [98304, 1], P(('dp', 'seq')), may hold values from 0 to 31; in each aligned block of 128 rows (0 to 127, 128 to 255, ...) at most 6 rows name the same one
- enc_group: int32 [98304], P(('dp', 'seq')), may hold values from 0 to 7
- query: bfloat16 [196608, 1024], P(('dp', 'seq')), may hold values from -12 to 12
- dec_group: int32 [196608], P(('dp', 'seq')), may hold values from 0 to 7
- out_grad: bfloat16 [196608, 1024], P(('dp', 'seq')), may hold values from -6 to 6
- w_kv: bfloat16 [2048, 2048], replicated, may hold values from -0.125 to 0.125
Outputs:
- query_grad: bfloat16 [196608, 1024], P(('dp', 'seq'))
- enc_grad: bfloat16 [98304, 2048], P(('dp', 'seq'))
- kv_weight_grad: float32 [2048, 2048], P('seq')
The draws below stay inside these ranges and needn't reach their ends.
Inputs may be any that keep to these rules, and one draw needn't show every extreme that they name: `enc_dest`: of the 128 encoder tokens of one device, at most 6 name any one decoder owner, and in every draw some owner is named by exactly 6 of them.
All inputs are finite; a program needn't handle non-finite values.
Results may differ from the reference program's by a relative error of at most 0.02.
Values may be sent and summed in bfloat16 or wider, within the bound.
No kernel may reach another device: no remote copies, remote signals or barrier semaphores. Data moves between devices by JAX's collectives and lax.ppermute only.
A program may use at most 64 MiB of HBM per device.

```python
import math
import jax
import jax.numpy as jnp
import numpy as np
from jax import lax

D = 2048
HEADS = 8
HEAD_DIM = 128
GROUPS = 8
ENC_DEV = 128
DEC_DEV = 256
HW = 1024
CAP = 6
SLOTS = 192
ENC_TOTAL = 98304
DEC_TOTAL = 196608
N_DP = 24
N_SEQ = 32


def draw_query(key, part):
    key = jax.random.fold_in(key, 7)
    return jnp.clip(jax.random.normal(key, (DEC_TOTAL, HW), jnp.float32), -6.0, 6.0).astype(jnp.bfloat16)


def place_ends(values, rng, smallest, top_value):
    longest = values.shape.index(max(values.shape))
    spots = []
    for shift in (0, 1):
        where = [jax.random.randint(jax.random.fold_in(rng, axis), (), 0, length) for axis, length in enumerate(values.shape)]
        where[longest] = (where[longest] + shift) % values.shape[longest]
        spots.append(tuple(where))
    return values.at[spots[0]].set(smallest).at[spots[1]].set(top_value)


def block_scale(own_key, shape, cuts, smallest, largest):
    def one(position, shards_of):
        heights = jax.random.uniform(jax.random.fold_in(jax.random.fold_in(own_key, 6), position), (shards_of,), jnp.float32, smallest / len(cuts), largest / len(cuts))
        return jnp.repeat(jnp.exp(heights), shape[position] // shards_of).reshape((-1,) + (1,) * (len(shape) - position - 1))

    loudness = one(*cuts[0])
    for cut in cuts[1:]:
        loudness = loudness * one(*cut)
    return loudness


def routed_block(rng, own, number, rows, amount, top, bound, slope):
    ranking = jax.random.permutation(rng, amount)
    packed, ordinary = portions_of(amount, rows * top, bound, slope, True), portions_of(amount, rows * top, bound, slope, False)
    places = jnp.arange(amount)

    def named(sizes, turn):
        used = int((sizes > 0).sum())
        fixed = max(1, used // 4)
        moved = fixed + (places - fixed + turn * (used - fixed)) % max(1, amount - fixed)
        return jnp.zeros((amount,), jnp.int32).at[ranking[jnp.where(places < fixed, places, moved)]].set(jnp.asarray(sizes, jnp.int32))

    sizes = jnp.where(number % 4 == 0, named(packed, number // 4), named(ordinary, number - number // 4 - 1))
    mixed = jax.random.permutation(jax.random.fold_in(own, 3), amount)
    donor, taker = mixed[0:amount // 2 * 2:2], mixed[1:amount // 2 * 2:2]
    margin = jnp.minimum(sizes[donor] - 1, bound - sizes[taker]) // 2
    margin = jnp.where((donor == ranking[0]) | (taker == ranking[0]) | (sizes[taker] == 0), 0, jnp.maximum(margin, 0))
    moved = jax.random.randint(jax.random.fold_in(own, 4), (amount // 2,), 0, 1 << 20) % (margin + 1)
    sizes = sizes.at[donor].add(-moved).at[taker].add(moved)
    members = jnp.searchsorted(jnp.cumsum(sizes), jnp.arange(rows * top), side="right").astype(jnp.int32)
    listing = members.reshape(top, rows).T
    listing = listing[jax.random.permutation(jax.random.fold_in(own, 1), rows)]
    turn = jax.random.randint(jax.random.fold_in(own, 2), (rows, 1), 0, top)
    return jnp.take_along_axis(listing, (jnp.arange(top)[None, :] + turn) % top, axis=1)


def portions_of(amount, total, reach, slope, full):
    weights = [(1 << 20) // math.isqrt(rank ** slope) + 1 for rank in range(1, amount + 1)]
    largest = reach if full else min(reach, max(-(-total // amount), total * weights[0] // sum(weights)))
    least = 1 if total - largest >= amount - 1 else 0
    counts, rest = [largest] + [least] * (amount - 1), total - largest - least * (amount - 1)
    while rest > 0:
        movable = [i for i in range(1, amount) if counts[i] < largest] or [i for i in range(1, amount) if counts[i] < reach]
        whole, left = sum([weights[i] for i in movable]), rest
        for i in movable:
            extra = min(reach - counts[i], max(1, left * weights[i] // whole), rest)
            counts[i] = counts[i] + extra
            rest = rest - extra
    return np.array(counts)


def scatter_about(key, extent, width, most, pieces=(), kind=jnp.bfloat16):
    drawn = width * jax.random.normal(key, extent, jnp.float32)
    if pieces:
        drawn = drawn * block_scale(key, extent, pieces, -0.22, 0.18)
    return jnp.clip(drawn, -most, most).astype(kind)


def setup_inputs(seed: int = 0) -> dict:
    splits = jax.random.split(jax.random.key(seed), 8)
    enc = scatter_about(splits[0], (ENC_TOTAL, D), 1.0, 6.0, ((0, 768),))
    enc_dest_keys = jax.random.split(jax.random.fold_in(splits[1], 1), ENC_TOTAL // ENC_DEV)
    enc_dest_turns = jax.random.permutation(jax.random.fold_in(splits[1], 3), ENC_TOTAL // ENC_DEV)
    enc_dest = jax.vmap(lambda own, number: routed_block(jax.random.fold_in(splits[1], 2), own, number, ENC_DEV, N_SEQ, 1, CAP, 2))(enc_dest_keys, enc_dest_turns).reshape((ENC_TOTAL, 1))
    enc_group = place_ends(jax.random.randint(splits[2], (ENC_TOTAL,), 0, GROUPS), jax.random.fold_in(splits[2], 1), 0, GROUPS - 1).astype(jnp.int32)
    query = draw_query(jax.random.fold_in(splits[7], 71), 0)
    dec_group = place_ends(jax.random.randint(splits[4], (DEC_TOTAL,), 0, GROUPS), jax.random.fold_in(splits[4], 1), 0, GROUPS - 1).astype(jnp.int32)
    out_grad = scatter_about(splits[5], (DEC_TOTAL, HW), 1.0, 6.0, ((0, 768),))
    w_kv = scatter_about(splits[6], (D, 2 * HW), D ** -0.5, 0.125)
    return {"enc": enc, "enc_dest": enc_dest, "enc_group": enc_group, "query": query, "dec_group": dec_group, "out_grad": out_grad, "w_kv": w_kv}


def attend(query_rows, grad_rows, groups, slot_kv, labels):
    scale = 1.0 / math.sqrt(HEAD_DIM)
    qf = query_rows.astype(jnp.float32).reshape(DEC_DEV, HEADS, HEAD_DIM)
    dof = grad_rows.astype(jnp.float32).reshape(DEC_DEV, HEADS, HEAD_DIM)
    keys = slot_kv[:, :HW].astype(jnp.float32).reshape(SLOTS, HEADS, HEAD_DIM)
    values = slot_kv[:, HW:].astype(jnp.float32).reshape(SLOTS, HEADS, HEAD_DIM)
    score = jnp.einsum('thd,rhd->htr', qf, keys) * scale
    allowed = (labels[None, :] == groups[:, None] + 1)[None]
    top = jnp.maximum(lax.optimization_barrier(jnp.max(jnp.where(allowed, score, 0.0), axis=-1, keepdims=True)), 0.0)
    expo = jnp.where(allowed, jnp.exp(score - top), 0.0)
    weight = expo / (jnp.exp(-top) + lax.optimization_barrier(jnp.sum(expo, axis=-1, keepdims=True)))
    probs = lax.optimization_barrier(weight.astype(jnp.bfloat16)).astype(jnp.float32)
    attended = jnp.einsum('htr,rhd->thd', probs, values)
    delta = jnp.einsum('thd,thd->ht', dof, attended)
    value_dot = jnp.einsum('thd,rhd->htr', dof, values)
    score_grad = weight * (value_dot - delta[:, :, None]) * scale
    score_grad = lax.optimization_barrier(score_grad.astype(jnp.bfloat16)).astype(jnp.float32)
    query_grad = jnp.einsum('htr,rhd->thd', score_grad, keys).reshape(DEC_DEV, HW).astype(jnp.bfloat16)
    key_grad = jnp.einsum('htr,thd->rhd', score_grad, qf).reshape(SLOTS, HW)
    value_grad = jnp.einsum('htr,thd->rhd', probs, dof).reshape(SLOTS, HW)
    slot_grad = jnp.concatenate([key_grad, value_grad], axis=1).astype(jnp.bfloat16)
    return (query_grad, slot_grad)

def reference(enc, enc_dest, enc_group, query, dec_group, out_grad, w_kv):
    devices = N_DP * N_SEQ
    norm_factor = 1.0 / math.sqrt(ENC_TOTAL)
    kv = jnp.dot(enc, w_kv, preferred_element_type=jnp.float32).astype(jnp.bfloat16)
    dest = enc_dest[:, 0].astype(jnp.int32)
    hits = (dest[:, None] == jnp.arange(N_SEQ, dtype=jnp.int32)[None, :]).astype(jnp.int32)
    hits = hits.reshape(devices, ENC_DEV, N_SEQ)
    before = jnp.cumsum(hits, axis=1).astype(jnp.int32) - hits
    rank = lax.optimization_barrier(jnp.sum(before * hits, axis=2)).reshape(-1).astype(jnp.int32)
    rows = jnp.arange(ENC_TOTAL, dtype=jnp.int32)
    source = rows // ENC_DEV % N_SEQ
    target = rows // (ENC_DEV * N_SEQ) * N_SEQ + dest
    slot = (source * CAP + rank).astype(jnp.int32)
    received = jnp.zeros((devices, SLOTS, 2 * HW), jnp.bfloat16).at[target, slot].set(kv)
    labels = jnp.zeros((devices, SLOTS), jnp.int32).at[target, slot].set(enc_group.astype(jnp.int32) + 1)
    query_grad, slot_grad = lax.map(lambda item: attend(*item), (query.reshape(devices, DEC_DEV, HW), out_grad.reshape(devices, DEC_DEV, HW), dec_group.astype(jnp.int32).reshape(devices, DEC_DEV), received, labels))
    kv_grad = slot_grad[target, slot]
    enc_grad = lax.dot_general(kv_grad, w_kv, (((1,), (1,)), ((), ())), preferred_element_type=jnp.float32).astype(jnp.bfloat16)

    def accumulate(total, item):
        block_rows, block_grad = item
        partial_value = lax.dot_general(block_rows, block_grad, (((0,), (0,)), ((), ())), preferred_element_type=jnp.float32) * norm_factor
        return (total + lax.optimization_barrier(partial_value.astype(jnp.bfloat16)).astype(jnp.float32), None)
    kv_weight_grad, unused = lax.scan(accumulate, jnp.zeros((D, 2 * HW), jnp.float32), (enc.reshape(devices, ENC_DEV, D), kv_grad.reshape(devices, ENC_DEV, 2 * HW)))
    return (query_grad.reshape(DEC_TOTAL, HW), enc_grad, kv_weight_grad)
```

```python
import math

import jax
import jax.numpy as jnp
from jax import lax
from jax.sharding import PartitionSpec as P

HEADS = 8
HEAD_DIM = 128
LANES = 128


def shards(enc, enc_dest, enc_group, query, dec_group, out_grad, w_kv):
    peers = lax.axis_size("seq")
    groups = lax.axis_size("dp")
    enc_rows, model = enc.shape
    capacity = 3 * enc_rows // (2 * peers)
    slot_count = peers * capacity
    full = w_kv.shape[1]
    width = full // 2
    dec_rows = query.shape[0]
    scale = 1.0 / math.sqrt(HEAD_DIM)
    norm_factor = 1.0 / math.sqrt(enc_rows * peers * groups)
    block = -(-full // (groups * 8)) * 8
    share = model // peers
    packed_rows = capacity * model // LANES

    enc_all = lax.all_gather(enc, "dp", axis=0, tiled=True)

    dest = enc_dest[:, 0]
    hits = (dest[:, None] == jnp.arange(peers, dtype=jnp.int32)[None, :]).astype(jnp.int32)
    before = jnp.cumsum(hits, axis=0) - hits
    rank = jnp.sum(before * hits, axis=1)
    target = dest * capacity + rank
    placed = target[:, None] == jnp.arange(slot_count, dtype=jnp.int32)[None, :]
    placing = placed.astype(jnp.bfloat16)
    slots = lax.dot_general(
        placing, enc, (((0,), (0,)), ((), ())), preferred_element_type=jnp.float32
    ).astype(jnp.bfloat16)
    label_out = jnp.sum(jnp.where(placed, (enc_group + 1)[:, None], 0), axis=0)
    label_out = label_out.astype(jnp.bfloat16).reshape(peers, 1, capacity)
    label_out = jnp.pad(label_out, ((0, 0), (0, 7), (0, LANES - capacity)))
    outgoing = jnp.concatenate([slots.reshape(peers, packed_rows, LANES), label_out], axis=1)
    incoming = lax.all_to_all(outgoing, "seq", split_axis=0, concat_axis=0, tiled=True)
    received = incoming[:, :packed_rows].reshape(slot_count, model)
    labels = incoming[:, packed_rows, :capacity].reshape(slot_count).astype(jnp.float32)

    slot_kv = jnp.dot(received, w_kv, preferred_element_type=jnp.float32).astype(jnp.bfloat16)
    allowed = (labels[None, :] == (dec_group + 1).astype(jnp.float32)[:, None])[None]
    queries = query.reshape(dec_rows, HEADS, HEAD_DIM)
    grads_in = out_grad.reshape(dec_rows, HEADS, HEAD_DIM)
    keys = slot_kv[:, :width].reshape(slot_count, HEADS, HEAD_DIM)
    values = slot_kv[:, width:].reshape(slot_count, HEADS, HEAD_DIM)
    score = jnp.einsum("thd,rhd->htr", queries, keys, preferred_element_type=jnp.float32) * scale
    top = jnp.maximum(jnp.max(jnp.where(allowed, score, 0.0), axis=-1, keepdims=True), 0.0)
    expo = jnp.where(allowed, jnp.exp(score - top), 0.0)
    weight = expo / (jnp.exp(-top) + jnp.sum(expo, axis=-1, keepdims=True))
    probs = weight.astype(jnp.bfloat16)
    attended = jnp.einsum("htr,rhd->thd", probs, values, preferred_element_type=jnp.float32)
    delta = jnp.sum(grads_in.astype(jnp.float32) * attended, axis=2).T
    value_dot = jnp.einsum("thd,rhd->htr", grads_in, values, preferred_element_type=jnp.float32)
    score_grad = (weight * (value_dot - delta[:, :, None]) * scale).astype(jnp.bfloat16)
    query_grad = (
        jnp.einsum("htr,rhd->thd", score_grad, keys, preferred_element_type=jnp.float32)
        .reshape(dec_rows, width)
        .astype(jnp.bfloat16)
    )
    key_grad = jnp.einsum(
        "htr,thd->rhd", score_grad, queries, preferred_element_type=jnp.float32
    ).reshape(slot_count, width)
    value_grad = jnp.einsum(
        "htr,thd->rhd", probs, grads_in, preferred_element_type=jnp.float32
    ).reshape(slot_count, width)
    slot_grad = jnp.concatenate([key_grad, value_grad], axis=1).astype(jnp.bfloat16)
    returned = lax.all_to_all(
        slot_grad.reshape(peers, packed_rows, LANES), "seq", split_axis=0, concat_axis=0, tiled=True
    ).reshape(slot_count, full)

    columns = lax.dot_general(
        returned, placing, (((0,), (1,)), ((), ())), preferred_element_type=jnp.float32
    ).astype(jnp.bfloat16)
    enc_grad = lax.dot_general(
        columns, w_kv, (((0,), (1,)), ((), ())), preferred_element_type=jnp.float32
    ).astype(jnp.bfloat16)

    blocks = jnp.pad(columns, ((0, groups * block - full), (0, 0))).reshape(groups, block, enc_rows)
    blocks = lax.all_to_all(blocks, "dp", split_axis=0, concat_axis=0, tiled=True)
    blocks = blocks.transpose(1, 0, 2).reshape(block, groups * enc_rows)
    part = jnp.dot(blocks, enc_all, preferred_element_type=jnp.float32) * norm_factor
    part = part.astype(jnp.bfloat16).reshape(2, block // 2, peers, share)
    part = part.transpose(2, 1, 0, 3).reshape(peers, block // 2, 2 * share)
    parts = lax.all_to_all(part, "seq", split_axis=0, concat_axis=0, tiled=True)
    total = jnp.sum(parts.astype(jnp.float32), axis=0).astype(jnp.bfloat16)
    totals = lax.all_gather(total, "dp", axis=0, tiled=False)
    totals = totals.reshape(groups, block // 2, 2, share).transpose(3, 0, 2, 1)
    kv_weight_grad = totals.reshape(share, groups * block)[:, :full].astype(jnp.float32)
    return (query_grad, enc_grad, kv_weight_grad)


def solution(mesh):
    in_specs = (
        P(("dp", "seq"), None),
        P(("dp", "seq"), None),
        P(("dp", "seq")),
        P(("dp", "seq"), None),
        P(("dp", "seq")),
        P(("dp", "seq"), None),
        P(),
    )
    out_specs = (P(("dp", "seq"), None), P(("dp", "seq"), None), P("seq", None))
    return jax.shard_map(shards, mesh=mesh, in_specs=in_specs, out_specs=out_specs, check_vma=False)
```

```python
import functools
import math

import jax
import jax.numpy as jnp
from jax import lax
from jax.experimental import pallas as pl
from jax.experimental.pallas import tpu as pltpu
from jax.sharding import Mesh, PartitionSpec as P

HEADS = 8
HEAD_DIM = 128
LANES = 128
FAR = -1e30
MIB = 1 << 20
IN_FLIGHT = 16
PARTS = 3


def contract(a, b, dims):
    return lax.dot_general(a, b, (dims, ((), ())), preferred_element_type=jnp.float32)


def streamed(source, target, sems):
    count = sems.shape[0]
    rows = source.shape[0] // count
    spans = [pl.ds(k * rows, rows) for k in range(count)]
    copies = [
        pltpu.make_async_copy(source.at[at], target.at[at], sems.at[k]) for k, at in enumerate(spans)
    ]
    for copy in copies[:IN_FLIGHT]:
        copy.start()

    def wait(k):
        copies[k].wait()
        if k + IN_FLIGHT < count:
            copies[k + IN_FLIGHT].start()

    return wait


def product(rows, source, near, sems, total):
    count = sems.shape[0]
    depth = source.shape[0] // count
    wait = streamed(source, near, sems)

    def run():
        for k in range(count):
            wait(k)
            at = slice(k * depth, (k + 1) * depth)
            part = contract(rows[:, at], near[at, :], ((1,), (0,)))
            total[...] = part if k == 0 else total[...] + part

    return run


def turned(row, diagonal):
    return jnp.sum(jnp.where(diagonal, row.astype(jnp.float32), 0.0), axis=1, keepdims=True)


def route_kernel(
    peers,
    capacity,
    stride,
    enc_hbm,
    dest_hbm,
    group_hbm,
    w_hbm,
    out_ref,
    placing_ref,
    enc_ref,
    row_refs,
    w_ref,
    kv,
    wide,
    sems,
    w_sems,
):
    copies = [
        pltpu.make_async_copy(dest_hbm, row_refs.at[0], sems.at[0]),
        pltpu.make_async_copy(group_hbm, row_refs.at[1], sems.at[1]),
        pltpu.make_async_copy(enc_hbm, enc_ref, sems.at[2]),
    ]
    for copy in copies:
        copy.start()
    multiply = product(enc_ref, w_hbm, w_ref, w_sems, kv)
    rows = enc_ref.shape[0]
    chunks = kv.shape[1] // LANES
    ahead = lax.broadcasted_iota(jnp.int32, (rows, rows), 0)
    behind = lax.broadcasted_iota(jnp.int32, (rows, rows), 1)
    earlier = jnp.where(behind < ahead, 1.0, 0.0).astype(jnp.bfloat16)
    copies[0].wait()
    copies[1].wait()
    dest = turned(row_refs[0], ahead == behind).astype(jnp.int32)
    label = turned(row_refs[1] + 1, ahead == behind)
    owner = lax.broadcasted_iota(jnp.int32, (rows, peers), 1)
    hits = jnp.where(owner == dest, 1.0, 0.0)
    before = contract(earlier, hits.astype(jnp.bfloat16), ((1,), (0,)))
    rank = jnp.sum(before * hits, axis=1, keepdims=True).astype(jnp.int32)
    slot = lax.broadcasted_iota(jnp.int32, (rows, peers * capacity), 1)
    placing_ref[...] = jnp.where(slot == dest * capacity + rank, 1.0, 0.0).astype(jnp.bfloat16)
    placing = jnp.where(slot == rank * peers + dest, 1.0, 0.0).astype(jnp.bfloat16)
    lane = lax.broadcasted_iota(jnp.int32, (rows, LANES), 1)
    spots = jnp.where(lane == rank, label, 0.0).astype(jnp.bfloat16)
    labels = contract(hits.astype(jnp.bfloat16), spots, ((0,), (0,)))
    for extra in range(capacity * chunks, stride):
        wide[pl.ds(extra, peers, stride=stride), :] = labels
    copies[2].wait()
    multiply()
    slots = contract(placing, kv[...].astype(jnp.bfloat16), ((0,), (0,)))
    for r in range(capacity):
        for c in range(chunks):
            wide[pl.ds(r * chunks + c, peers, stride=stride), :] = slots[
                r * peers : (r + 1) * peers, c * LANES : (c + 1) * LANES
            ]
    out_ref[...] = wide[...].astype(jnp.bfloat16)


def attention_kernel(
    peers,
    capacity,
    stride,
    incoming_ref,
    group_ref,
    placing_ref,
    query_ref,
    grad_ref,
    query_grad_ref,
    out_ref,
    placing_out_ref,
    wide,
    received,
    bias,
):
    slot_count, model = received.shape
    chunks = model // LANES
    width = HEADS * HEAD_DIM
    scale = 1.0 / math.sqrt(HEAD_DIM)
    placing_out_ref[...] = placing_ref[...]
    wide[...] = incoming_ref[...].astype(jnp.float32)
    for r in range(capacity):
        for c in range(chunks):
            received[r * peers : (r + 1) * peers, c * LANES : (c + 1) * LANES] = wide[
                pl.ds(r * chunks + c, peers, stride=stride), :
            ].astype(jnp.bfloat16)
    labels = wide[pl.ds(capacity * chunks, peers, stride=stride), :]
    group = group_ref[...].astype(jnp.float32) + 1.0
    for r in range(capacity):
        bias[r * peers : (r + 1) * peers, :] = jnp.where(labels[:, r : r + 1] == group, 0.0, FAR)

    def columns_of(head):
        return slice(head * HEAD_DIM, (head + 1) * HEAD_DIM)

    def products(head):
        at, of_values = columns_of(head), columns_of(HEADS + head)
        score = contract(received[:, at], query_ref[:, at], ((1,), (1,))) * scale + bias[...]
        value_dot = contract(received[:, of_values], grad_ref[:, at], ((1,), (1,)))
        return score, value_dot

    def softmax(score, value_dot):
        top = jnp.maximum(jnp.max(score, axis=0, keepdims=True), 0.0)
        expo = jnp.exp(score - top)
        weight = expo * (1.0 / (jnp.exp(-top) + jnp.sum(expo, axis=0, keepdims=True)))
        probs = weight.astype(jnp.bfloat16)
        delta = jnp.sum(probs.astype(jnp.float32) * value_dot, axis=0, keepdims=True)
        return probs, (weight * ((value_dot - delta) * scale)).astype(jnp.bfloat16)

    def gradients(head, probs, score_grad):
        at = columns_of(head)
        key_grad = contract(score_grad, query_ref[:, at], ((1,), (0,)))
        value_grad = contract(probs, grad_ref[:, at], ((1,), (0,)))
        query_grad_ref[:, at] = contract(score_grad, received[:, at], ((0,), (0,))).astype(jnp.bfloat16)
        for r in range(capacity):
            rows = slice(r * peers, (r + 1) * peers)
            for c, part in ((head, key_grad), (HEADS + head, value_grad)):
                wide[pl.ds(r * chunks + c, peers, stride=capacity * chunks), :] = part[rows]

    scores, weights = {}, {}
    for turn in range(HEADS + 2):
        if turn < HEADS:
            scores[turn] = products(turn)
        if 0 <= turn - 1 < HEADS:
            weights[turn - 1] = softmax(*scores.pop(turn - 1))
        if turn >= 2:
            gradients(turn - 2, *weights.pop(turn - 2))
    out_ref[...] = wide[: slot_count * chunks, :].astype(jnp.bfloat16)


def columns_kernel(returned_ref, placing_ref, out_ref, wide):
    wide[...] = returned_ref[...].astype(jnp.float32)
    slot_count = placing_ref.shape[1]
    chunks = returned_ref.shape[0] // slot_count
    for c in range(chunks):
        rows = wide[pl.ds(c, slot_count, stride=chunks), :].astype(jnp.bfloat16)
        turned_rows = contract(rows, placing_ref[...], ((0,), (1,)))
        out_ref[c * LANES : (c + 1) * LANES, :] = turned_rows.astype(jnp.bfloat16)
    extra = out_ref.shape[0] - chunks * LANES
    if extra:
        out_ref[chunks * LANES :, :] = jnp.zeros((extra, out_ref.shape[1]), jnp.bfloat16)


def tile_kernel(block, share, norm_factor, blocks_ref, enc_hbm, out_ref, rows, near, total, sems):
    multiply = product(rows, enc_hbm, near, sems, total)
    groups, enc_rows = blocks_ref.shape[0], blocks_ref.shape[2]
    for g in range(groups):
        rows[:, g * enc_rows : (g + 1) * enc_rows] = blocks_ref[g]
    multiply()
    kept = out_ref.shape[1]
    low = lax.broadcasted_iota(jnp.int32, (kept, LANES), 1) < share
    for p in range(total.shape[1] // LANES):
        two = total[:, p * LANES : (p + 1) * LANES] * norm_factor
        first, second = two[:kept], two[block - kept :]
        out_ref[2 * p] = jnp.where(low, first, pltpu.roll(second, share, 1)).astype(jnp.bfloat16)
        out_ref[2 * p + 1] = jnp.where(low, pltpu.roll(first, share, 1), second).astype(jnp.bfloat16)


def sum_kernel(block, share, parts_ref, out_ref):
    kept = parts_ref.shape[1]
    total = parts_ref[0].astype(jnp.float32)
    for i in range(1, parts_ref.shape[0]):
        total += parts_ref[i].astype(jnp.float32)
    columns = total.T
    pieces = [columns[:share], columns[share:, 2 * kept - block :]]
    extra = out_ref.shape[1] - block
    if extra:
        pieces.append(jnp.zeros((share, extra), jnp.float32))
    out_ref[...] = jnp.concatenate(pieces, axis=1).astype(jnp.bfloat16)


def join_kernel(totals_ref, out_ref):
    total = totals_ref[0].astype(jnp.float32)
    for t in range(1, totals_ref.shape[0]):
        total += totals_ref[t].astype(jnp.float32)
    shared = total.astype(jnp.bfloat16)
    for g in range(out_ref.shape[0]):
        out_ref[g] = shared


def final_kernel(block, totals_ref, out_ref):
    full = out_ref.shape[1]
    for g in range(totals_ref.shape[0]):
        end = min((g + 1) * block, full)
        out_ref[:, g * block : end] = totals_ref[g, :, : end - g * block].astype(jnp.float32)


def shards(enc, enc_dest, enc_group, query, dec_group, out_grad, w_kv):
    peers = lax.axis_size("seq")
    parts = lax.axis_size("part")
    groups = lax.axis_size("group")
    enc_rows, model = enc.shape
    capacity = 3 * enc_rows // (2 * peers)
    slot_count = peers * capacity
    full = w_kv.shape[1]
    width = full // 2
    dec_rows = query.shape[0]
    norm_factor = 1.0 / math.sqrt(enc_rows * peers * groups * parts)
    block = -(-full // (groups * 8)) * 8
    kept = -(-block // 32) * 16
    block_lanes = -(-block // LANES) * LANES
    share = model // peers
    chunks = full // LANES
    packed_rows = capacity * chunks
    stride = packed_rows + 8

    enc_all = lax.all_gather(enc, "group", axis=0, tiled=True)

    outgoing, placing = pl.pallas_call(
        functools.partial(route_kernel, peers, capacity, stride),
        out_shape=(
            jax.ShapeDtypeStruct((peers * stride, LANES), jnp.bfloat16),
            jax.ShapeDtypeStruct((enc_rows, slot_count), jnp.bfloat16),
        ),
        in_specs=[pl.BlockSpec(memory_space=pltpu.HBM)] * 4,
        scratch_shapes=[
            pltpu.VMEM((enc_rows, model), jnp.bfloat16),
            pltpu.VMEM((2, 1, enc_rows), jnp.int32),
            pltpu.VMEM((model, full), jnp.bfloat16),
            pltpu.VMEM((enc_rows, full), jnp.float32),
            pltpu.VMEM((peers * stride, LANES), jnp.float32),
            pltpu.SemaphoreType.DMA((3,)),
            pltpu.SemaphoreType.DMA((4,)),
        ],
        compiler_params=pltpu.CompilerParams(vmem_limit_bytes=64 * MIB),
    )(enc, enc_dest.reshape(1, enc_rows), enc_group.reshape(1, enc_rows), w_kv)
    incoming = lax.all_to_all(
        outgoing.reshape(peers, stride, LANES), "seq", split_axis=0, concat_axis=0, tiled=True
    )

    query_grad, slot_grad, placing = pl.pallas_call(
        functools.partial(attention_kernel, peers, capacity, stride),
        out_shape=(
            jax.ShapeDtypeStruct((dec_rows, width), jnp.bfloat16),
            jax.ShapeDtypeStruct((peers * packed_rows, LANES), jnp.bfloat16),
            jax.ShapeDtypeStruct((enc_rows, slot_count), jnp.bfloat16),
        ),
        scratch_shapes=[
            pltpu.VMEM((peers * stride, LANES), jnp.float32),
            pltpu.VMEM((slot_count, full), jnp.bfloat16),
            pltpu.VMEM((slot_count, dec_rows), jnp.float32),
        ],
        compiler_params=pltpu.CompilerParams(vmem_limit_bytes=60 * MIB),
    )(
        incoming.reshape(peers * stride, LANES),
        dec_group.reshape(1, dec_rows),
        placing,
        query,
        out_grad,
    )
    returned = lax.all_to_all(
        slot_grad.reshape(peers, packed_rows, LANES), "seq", split_axis=0, concat_axis=0, tiled=True
    )

    columns = pl.pallas_call(
        columns_kernel,
        out_shape=jax.ShapeDtypeStruct((groups * block, enc_rows), jnp.bfloat16),
        scratch_shapes=[pltpu.VMEM((peers * packed_rows, LANES), jnp.float32)],
        compiler_params=pltpu.CompilerParams(vmem_limit_bytes=32 * MIB),
    )(returned.reshape(peers * packed_rows, LANES), placing)
    enc_grad = contract(columns[:full], w_kv, ((0,), (1,))).astype(jnp.bfloat16)

    blocks = lax.all_to_all(
        columns.reshape(groups, block, enc_rows), "group", split_axis=0, concat_axis=0, tiled=True
    )
    tile = pl.pallas_call(
        functools.partial(tile_kernel, block, share, norm_factor),
        out_shape=jax.ShapeDtypeStruct((peers, kept, 2 * share), jnp.bfloat16),
        in_specs=[pl.BlockSpec(memory_space=pltpu.VMEM), pl.BlockSpec(memory_space=pltpu.HBM)],
        scratch_shapes=[
            pltpu.VMEM((block, groups * enc_rows), jnp.bfloat16),
            pltpu.VMEM((groups * enc_rows, model), jnp.bfloat16),
            pltpu.VMEM((block, model), jnp.float32),
            pltpu.SemaphoreType.DMA((groups // 2,)),
        ],
        compiler_params=pltpu.CompilerParams(vmem_limit_bytes=62 * MIB),
    )(blocks, enc_all)
    tiles = lax.all_to_all(tile, "seq", split_axis=0, concat_axis=0, tiled=True)
    shared = pl.pallas_call(
        functools.partial(sum_kernel, block, share),
        out_shape=jax.ShapeDtypeStruct((share, block_lanes), jnp.bfloat16),
        compiler_params=pltpu.CompilerParams(vmem_limit_bytes=32 * MIB),
    )(tiles)
    shared = lax.all_gather(shared, "part", axis=0, tiled=True).reshape(parts, share, block_lanes)
    shared = pl.pallas_call(
        join_kernel,
        out_shape=jax.ShapeDtypeStruct((groups, share, block_lanes), jnp.bfloat16),
        compiler_params=pltpu.CompilerParams(vmem_limit_bytes=32 * MIB),
    )(shared)
    shared = lax.all_to_all(shared, "group", split_axis=0, concat_axis=0, tiled=True)
    kv_weight_grad = pl.pallas_call(
        functools.partial(final_kernel, block),
        out_shape=jax.ShapeDtypeStruct((share, full), jnp.float32),
        compiler_params=pltpu.CompilerParams(vmem_limit_bytes=32 * MIB),
    )(shared)
    return (query_grad, enc_grad, kv_weight_grad)


def solution(mesh):
    dp, seq = mesh.devices.shape
    cut = Mesh(mesh.devices.reshape(PARTS, dp // PARTS, seq), ("part", "group", "seq"))
    rows = ("part", "group", "seq")
    in_specs = (P(rows, None), P(rows, None), P(rows), P(rows, None), P(rows), P(rows, None), P())
    out_specs = (P(rows, None), P(rows, None), P("seq", None))
    return jax.shard_map(shards, mesh=cut, in_specs=in_specs, out_specs=out_specs, check_vma=False)
```

```python
import functools
import math

import jax
import jax.numpy as jnp
from jax import lax
from jax.experimental import pallas as pl
from jax.experimental.pallas import tpu as pltpu
from jax.sharding import Mesh, PartitionSpec as P

HEADS = 8
HEAD_DIM = 128
LANES = 128
FAR = -1e30
MIB = 1 << 20
LINE = 4


def contract(a, b, dims):
    return lax.dot_general(a, b, (dims, ((), ())), preferred_element_type=jnp.float32)


def product(rows, sources, near, sems, total):
    count = sems.shape[0]
    depth = near.shape[0] // count
    each = count // len(sources)
    spans = [pl.ds(k * depth, depth) for k in range(count)]
    copies = [
        pltpu.make_async_copy(sources[k // each].at[spans[k % each]], near.at[spans[k]], sems.at[k])
        for k in range(count)
    ]
    for copy in copies:
        copy.start()

    def run():
        for k in range(count):
            copies[k].wait()
            at = slice(k * depth, (k + 1) * depth)
            part = contract(rows[:, at], near[at, :], ((1,), (0,)))
            total[...] = part if k == 0 else total[...] + part

    return run


def turned(row, diagonal):
    return jnp.sum(jnp.where(diagonal, row.astype(jnp.float32), 0.0), axis=1, keepdims=True)


def route_kernel(
    peers,
    capacity,
    stride,
    enc_hbm,
    dest_hbm,
    group_hbm,
    w_hbm,
    out_ref,
    placing_ref,
    enc_ref,
    row_refs,
    w_ref,
    kv,
    wide,
    sems,
    w_sems,
):
    copies = [
        pltpu.make_async_copy(dest_hbm, row_refs.at[0], sems.at[0]),
        pltpu.make_async_copy(group_hbm, row_refs.at[1], sems.at[1]),
        pltpu.make_async_copy(enc_hbm, enc_ref, sems.at[2]),
    ]
    for copy in copies:
        copy.start()
    multiply = product(enc_ref, [w_hbm], w_ref, w_sems, kv)
    rows = enc_ref.shape[0]
    chunks = kv.shape[1] // LANES
    ahead = lax.broadcasted_iota(jnp.int32, (rows, rows), 0)
    behind = lax.broadcasted_iota(jnp.int32, (rows, rows), 1)
    earlier = jnp.where(behind < ahead, 1.0, 0.0).astype(jnp.bfloat16)
    copies[0].wait()
    copies[1].wait()
    dest = turned(row_refs[0], ahead == behind).astype(jnp.int32)
    label = turned(row_refs[1] + 1, ahead == behind)
    owner = lax.broadcasted_iota(jnp.int32, (rows, peers), 1)
    hits = jnp.where(owner == dest, 1.0, 0.0)
    before = contract(earlier, hits.astype(jnp.bfloat16), ((1,), (0,)))
    rank = jnp.sum(before * hits, axis=1, keepdims=True).astype(jnp.int32)
    slot = lax.broadcasted_iota(jnp.int32, (rows, peers * capacity), 1)
    placing_ref[...] = jnp.where(slot == dest * capacity + rank, 1.0, 0.0).astype(jnp.bfloat16)
    placing = jnp.where(slot == rank * peers + dest, 1.0, 0.0).astype(jnp.bfloat16)
    lane = lax.broadcasted_iota(jnp.int32, (rows, LANES), 1)
    spots = jnp.where(lane == rank, label, 0.0).astype(jnp.bfloat16)
    labels = contract(hits.astype(jnp.bfloat16), spots, ((0,), (0,)))
    for extra in range(capacity * chunks, stride):
        wide[pl.ds(extra, peers, stride=stride), :] = labels
    copies[2].wait()
    multiply()
    slots = contract(placing, kv[...].astype(jnp.bfloat16), ((0,), (0,)))
    for r in range(capacity):
        for c in range(chunks):
            wide[pl.ds(r * chunks + c, peers, stride=stride), :] = slots[
                r * peers : (r + 1) * peers, c * LANES : (c + 1) * LANES
            ]
    out_ref[...] = wide[...].astype(jnp.bfloat16)


def attention_kernel(
    peers,
    capacity,
    stride,
    incoming_ref,
    group_ref,
    placing_ref,
    query_ref,
    grad_ref,
    query_grad_ref,
    out_ref,
    placing_out_ref,
    wide,
    received,
    bias,
):
    slot_count, model = received.shape
    chunks = model // LANES
    width = HEADS * HEAD_DIM
    scale = 1.0 / math.sqrt(HEAD_DIM)
    placing_out_ref[...] = placing_ref[...]
    wide[...] = incoming_ref[...].astype(jnp.float32)
    for r in range(capacity):
        for c in range(chunks):
            received[r * peers : (r + 1) * peers, c * LANES : (c + 1) * LANES] = wide[
                pl.ds(r * chunks + c, peers, stride=stride), :
            ].astype(jnp.bfloat16)
    labels = wide[pl.ds(capacity * chunks, peers, stride=stride), :]
    group = group_ref[...].astype(jnp.float32) + 1.0
    for r in range(capacity):
        bias[r * peers : (r + 1) * peers, :] = jnp.where(labels[:, r : r + 1] == group, 0.0, FAR)

    def columns_of(head):
        return slice(head * HEAD_DIM, (head + 1) * HEAD_DIM)

    def products(head):
        at, of_values = columns_of(head), columns_of(HEADS + head)
        score = contract(received[:, at], query_ref[:, at], ((1,), (1,))) * scale + bias[...]
        value_dot = contract(received[:, of_values], grad_ref[:, at], ((1,), (1,)))
        return score, value_dot

    def softmax(score, value_dot):
        top = jnp.maximum(jnp.max(score, axis=0, keepdims=True), 0.0)
        expo = jnp.exp(score - top)
        weight = expo * (1.0 / (jnp.exp(-top) + jnp.sum(expo, axis=0, keepdims=True)))
        probs = weight.astype(jnp.bfloat16)
        delta = jnp.sum(probs.astype(jnp.float32) * value_dot, axis=0, keepdims=True)
        return probs, (weight * ((value_dot - delta) * scale)).astype(jnp.bfloat16)

    def gradients(head, probs, score_grad):
        at = columns_of(head)
        key_grad = contract(score_grad, query_ref[:, at], ((1,), (0,)))
        value_grad = contract(probs, grad_ref[:, at], ((1,), (0,)))
        query_grad_ref[:, at] = contract(score_grad, received[:, at], ((0,), (0,))).astype(jnp.bfloat16)
        for r in range(capacity):
            rows = slice(r * peers, (r + 1) * peers)
            for c, part in ((head, key_grad), (HEADS + head, value_grad)):
                wide[pl.ds(r * chunks + c, peers, stride=capacity * chunks), :] = part[rows]

    scores, weights = {}, {}
    for turn in range(HEADS + 2):
        if turn < HEADS:
            scores[turn] = products(turn)
        if 0 <= turn - 1 < HEADS:
            weights[turn - 1] = softmax(*scores.pop(turn - 1))
        if turn >= 2:
            gradients(turn - 2, *weights.pop(turn - 2))
    out_ref[...] = wide[: slot_count * chunks, :].astype(jnp.bfloat16)


def columns_kernel(returned_ref, placing_ref, out_ref, wide):
    wide[...] = returned_ref[...].astype(jnp.float32)
    slot_count = placing_ref.shape[1]
    chunks = returned_ref.shape[0] // slot_count
    for c in range(chunks):
        rows = wide[pl.ds(c, slot_count, stride=chunks), :].astype(jnp.bfloat16)
        turned_rows = contract(rows, placing_ref[...], ((0,), (1,)))
        out_ref[c * LANES : (c + 1) * LANES, :] = turned_rows.astype(jnp.bfloat16)
    extra = out_ref.shape[0] - chunks * LANES
    if extra:
        out_ref[chunks * LANES :, :] = jnp.zeros((extra, out_ref.shape[1]), jnp.bfloat16)


def tile_kernel(
    block, share, norm_factor, order_ref, blocks_ref, own_hbm, other_hbm, out_ref, rows, near, total, sems
):
    multiply = product(rows, [own_hbm, other_hbm], near, sems, total)
    groups, enc_rows = blocks_ref.shape[0], blocks_ref.shape[2]
    for k in range(groups):
        rows[:, k * enc_rows : (k + 1) * enc_rows] = blocks_ref[order_ref[k]]
    multiply()
    kept = out_ref.shape[1]
    low = lax.broadcasted_iota(jnp.int32, (kept, LANES), 1) < share
    for p in range(total.shape[1] // LANES):
        two = total[:, p * LANES : (p + 1) * LANES] * norm_factor
        first, second = two[:kept], two[block - kept :]
        out_ref[2 * p] = jnp.where(low, first, pltpu.roll(second, share, 1)).astype(jnp.bfloat16)
        out_ref[2 * p + 1] = jnp.where(low, pltpu.roll(first, share, 1), second).astype(jnp.bfloat16)


def sum_kernel(block, share, parts_ref, out_ref):
    kept = parts_ref.shape[1]
    total = parts_ref[0].astype(jnp.float32)
    for i in range(1, parts_ref.shape[0]):
        total += parts_ref[i].astype(jnp.float32)
    columns = total.T
    out_ref[:, :kept] = columns[:share].astype(jnp.bfloat16)
    out_ref[:, kept:] = columns[share:, 2 * kept - block :].astype(jnp.bfloat16)


def final_kernel(block, totals_ref, out_ref):
    for g in range(totals_ref.shape[1]):
        total = totals_ref[0, g].astype(jnp.float32)
        for t in range(1, totals_ref.shape[0]):
            total += totals_ref[t, g].astype(jnp.float32)
        out_ref[:, g * block : (g + 1) * block] = total


def shards(enc, enc_dest, enc_group, query, dec_group, out_grad, w_kv):
    peers = lax.axis_size("seq")
    parts = lax.axis_size("part")
    line = lax.axis_size("line")
    groups = line * lax.axis_size("core")
    enc_rows, model = enc.shape
    capacity = 3 * enc_rows // (2 * peers)
    slot_count = peers * capacity
    full = w_kv.shape[1]
    width = full // 2
    dec_rows = query.shape[0]
    norm_factor = 1.0 / math.sqrt(enc_rows * peers * groups * parts)
    block = -(-full // (groups * 8)) * 8
    kept = -(-block // 32) * 16
    share = model // peers
    chunks = full // LANES
    packed_rows = capacity * chunks
    stride = packed_rows + 8

    outgoing, placing = pl.pallas_call(
        functools.partial(route_kernel, peers, capacity, stride),
        out_shape=(
            jax.ShapeDtypeStruct((peers * stride, LANES), jnp.bfloat16),
            jax.ShapeDtypeStruct((enc_rows, slot_count), jnp.bfloat16),
        ),
        in_specs=[pl.BlockSpec(memory_space=pltpu.HBM)] * 4,
        scratch_shapes=[
            pltpu.VMEM((enc_rows, model), jnp.bfloat16),
            pltpu.VMEM((2, 1, enc_rows), jnp.int32),
            pltpu.VMEM((model, full), jnp.bfloat16),
            pltpu.VMEM((enc_rows, full), jnp.float32),
            pltpu.VMEM((peers * stride, LANES), jnp.float32),
            pltpu.SemaphoreType.DMA((3,)),
            pltpu.SemaphoreType.DMA((4,)),
        ],
        compiler_params=pltpu.CompilerParams(vmem_limit_bytes=64 * MIB),
    )(enc, enc_dest.reshape(1, enc_rows), enc_group.reshape(1, enc_rows), w_kv)
    mine, outgoing = lax.optimization_barrier((enc, outgoing))
    passed = [lax.ppermute(mine, "line", [(i, i ^ k) for i in range(line)]) for k in range(1, line)]
    incoming = lax.all_to_all(
        outgoing.reshape(peers, stride, LANES), "seq", split_axis=0, concat_axis=0, tiled=True
    )

    query_grad, slot_grad, placing = pl.pallas_call(
        functools.partial(attention_kernel, peers, capacity, stride),
        out_shape=(
            jax.ShapeDtypeStruct((dec_rows, width), jnp.bfloat16),
            jax.ShapeDtypeStruct((peers * packed_rows, LANES), jnp.bfloat16),
            jax.ShapeDtypeStruct((enc_rows, slot_count), jnp.bfloat16),
        ),
        scratch_shapes=[
            pltpu.VMEM((peers * stride, LANES), jnp.float32),
            pltpu.VMEM((slot_count, full), jnp.bfloat16),
            pltpu.VMEM((slot_count, dec_rows), jnp.float32),
        ],
        compiler_params=pltpu.CompilerParams(vmem_limit_bytes=32 * MIB),
    )(
        incoming.reshape(peers * stride, LANES),
        dec_group.reshape(1, dec_rows),
        placing,
        query,
        out_grad,
    )
    *passed, _ = lax.optimization_barrier((*passed, slot_grad))
    own = jnp.concatenate([enc] + passed)
    other = lax.ppermute(own, "core", [(0, 1), (1, 0)])
    returned = lax.all_to_all(
        slot_grad.reshape(peers, packed_rows, LANES), "seq", split_axis=0, concat_axis=0, tiled=True
    )

    columns = pl.pallas_call(
        columns_kernel,
        out_shape=jax.ShapeDtypeStruct((groups * block, enc_rows), jnp.bfloat16),
        scratch_shapes=[pltpu.VMEM((peers * packed_rows, LANES), jnp.float32)],
        compiler_params=pltpu.CompilerParams(vmem_limit_bytes=32 * MIB),
    )(returned.reshape(peers * packed_rows, LANES), placing)
    enc_grad = contract(columns[:full], w_kv, ((0,), (1,))).astype(jnp.bfloat16)

    blocks = lax.all_to_all(
        columns.reshape(groups, block, enc_rows), ("line", "core"), split_axis=0, concat_axis=0, tiled=True
    )
    place = jnp.arange(groups, dtype=jnp.int32)
    order = (lax.axis_index("line") ^ place % line) * 2 + (lax.axis_index("core") ^ place // line)
    tile = pl.pallas_call(
        functools.partial(tile_kernel, block, share, norm_factor),
        out_shape=jax.ShapeDtypeStruct((peers, kept, 2 * share), jnp.bfloat16),
        in_specs=[
            pl.BlockSpec(memory_space=pltpu.SMEM),
            pl.BlockSpec(memory_space=pltpu.VMEM),
            pl.BlockSpec(memory_space=pltpu.HBM),
            pl.BlockSpec(memory_space=pltpu.HBM),
        ],
        scratch_shapes=[
            pltpu.VMEM((block, groups * enc_rows), jnp.bfloat16),
            pltpu.VMEM((groups * enc_rows, model), jnp.bfloat16),
            pltpu.VMEM((block, model), jnp.float32),
            pltpu.SemaphoreType.DMA((groups // 2,)),
        ],
        compiler_params=pltpu.CompilerParams(vmem_limit_bytes=32 * MIB),
    )(order, blocks, own, other)
    tiles = lax.all_to_all(tile, "seq", split_axis=0, concat_axis=0, tiled=True)
    shared = pl.pallas_call(
        functools.partial(sum_kernel, block, share),
        out_shape=jax.ShapeDtypeStruct((share, block), jnp.bfloat16),
        compiler_params=pltpu.CompilerParams(vmem_limit_bytes=32 * MIB),
    )(tiles)
    totals = lax.all_gather(shared, ("part", "line", "core"), axis=0, tiled=True)
    kv_weight_grad = pl.pallas_call(
        functools.partial(final_kernel, block),
        out_shape=jax.ShapeDtypeStruct((share, full), jnp.float32),
        compiler_params=pltpu.CompilerParams(vmem_limit_bytes=32 * MIB),
    )(totals.reshape(parts, groups, share, block))
    return (query_grad, enc_grad, kv_weight_grad)


def solution(mesh):
    dp, seq = mesh.devices.shape
    names = ("part", "line", "core", "seq")
    cut = Mesh(mesh.devices.reshape(dp // (2 * LINE), LINE, 2, seq), names)
    in_specs = (P(names, None), P(names, None), P(names), P(names, None), P(names), P(names, None), P())
    out_specs = (P(names, None), P(names, None), P("seq", None))
    return jax.shard_map(shards, mesh=cut, in_specs=in_specs, out_specs=out_specs, check_vma=False)
```

```python
import functools
import math

import jax
import jax.numpy as jnp
from jax import lax
from jax.experimental import pallas as pl
from jax.experimental.pallas import tpu as pltpu
from jax.sharding import Mesh, PartitionSpec as P

HEADS = 8
HEAD_DIM = 128
LANES = 128
FAR = -1e30
MIB = 1 << 20
LINE = 4


def contract(a, b, dims):
    return lax.dot_general(a, b, (dims, ((), ())), preferred_element_type=jnp.float32)


def product(rows, sources, near, sems, total):
    count = sems.shape[0]
    depth = near.shape[0] // count
    each = count // len(sources)
    spans = [pl.ds(k * depth, depth) for k in range(count)]
    copies = [
        pltpu.make_async_copy(sources[k // each].at[spans[k % each]], near.at[spans[k]], sems.at[k])
        for k in range(count)
    ]
    for copy in copies:
        copy.start()

    def run():
        for k in range(count):
            copies[k].wait()
            at = slice(k * depth, (k + 1) * depth)
            part = contract(rows[:, at], near[at, :], ((1,), (0,)))
            total[...] = part if k == 0 else total[...] + part

    return run


def turned(row, diagonal):
    return jnp.sum(jnp.where(diagonal, row.astype(jnp.float32), 0.0), axis=1, keepdims=True)


def route_kernel(
    peers,
    capacity,
    stride,
    enc_hbm,
    dest_hbm,
    group_hbm,
    w_hbm,
    out_ref,
    placing_ref,
    enc_ref,
    row_refs,
    w_ref,
    kv,
    wide,
    sems,
    w_sems,
):
    copies = [
        pltpu.make_async_copy(dest_hbm, row_refs.at[0], sems.at[0]),
        pltpu.make_async_copy(group_hbm, row_refs.at[1], sems.at[1]),
        pltpu.make_async_copy(enc_hbm, enc_ref, sems.at[2]),
    ]
    for copy in copies:
        copy.start()
    multiply = product(enc_ref, [w_hbm], w_ref, w_sems, kv)
    rows = enc_ref.shape[0]
    chunks = kv.shape[1] // LANES
    ahead = lax.broadcasted_iota(jnp.int32, (rows, rows), 0)
    behind = lax.broadcasted_iota(jnp.int32, (rows, rows), 1)
    earlier = jnp.where(behind < ahead, 1.0, 0.0).astype(jnp.bfloat16)
    copies[0].wait()
    copies[1].wait()
    dest = turned(row_refs[0], ahead == behind).astype(jnp.int32)
    label = turned(row_refs[1] + 1, ahead == behind)
    owner = lax.broadcasted_iota(jnp.int32, (rows, peers), 1)
    hits = jnp.where(owner == dest, 1.0, 0.0)
    before = contract(earlier, hits.astype(jnp.bfloat16), ((1,), (0,)))
    rank = jnp.sum(before * hits, axis=1, keepdims=True).astype(jnp.int32)
    slot = lax.broadcasted_iota(jnp.int32, (rows, peers * capacity), 1)
    placing_ref[...] = jnp.where(slot == dest * capacity + rank, 1.0, 0.0).astype(jnp.bfloat16)
    placing = jnp.where(slot == rank * peers + dest, 1.0, 0.0).astype(jnp.bfloat16)
    lane = lax.broadcasted_iota(jnp.int32, (rows, LANES), 1)
    spots = jnp.where(lane == rank, label, 0.0).astype(jnp.bfloat16)
    labels = contract(hits.astype(jnp.bfloat16), spots, ((0,), (0,)))
    for extra in range(capacity * chunks, stride):
        wide[pl.ds(extra, peers, stride=stride), :] = labels
    copies[2].wait()
    multiply()
    slots = contract(placing, kv[...].astype(jnp.bfloat16), ((0,), (0,)))
    for r in range(capacity):
        for c in range(chunks):
            wide[pl.ds(r * chunks + c, peers, stride=stride), :] = slots[
                r * peers : (r + 1) * peers, c * LANES : (c + 1) * LANES
            ]
    out_ref[...] = wide[...].astype(jnp.bfloat16)


def stage_kernel(count, *refs):
    sources, targets, sems = refs[:count], refs[-count - 1 : -1], refs[-1]
    copies = [
        pltpu.make_async_copy(source, target, sems.at[k])
        for k, (source, target) in enumerate(zip(sources, targets))
    ]
    for copy in copies:
        copy.start()
    for copy in copies:
        copy.wait()


def stage(arrays, after):
    count = len(arrays)
    return pl.pallas_call(
        functools.partial(stage_kernel, count),
        out_shape=tuple(jax.ShapeDtypeStruct(a.shape, a.dtype) for a in arrays),
        in_specs=[pl.BlockSpec(memory_space=pltpu.HBM)] * count + [pl.BlockSpec(memory_space=pl.ANY)],
        out_specs=tuple(pl.BlockSpec(memory_space=pltpu.VMEM) for a in arrays),
        scratch_shapes=[pltpu.SemaphoreType.DMA((count,))],
        compiler_params=pltpu.CompilerParams(vmem_limit_bytes=32 * MIB),
    )(*arrays, after)


def attention_kernel(
    peers,
    capacity,
    stride,
    incoming_ref,
    group_ref,
    query_ref,
    grad_ref,
    query_grad_ref,
    out_ref,
    wide,
    received,
    bias,
):
    slot_count, model = received.shape
    chunks = model // LANES
    width = HEADS * HEAD_DIM
    scale = 1.0 / math.sqrt(HEAD_DIM)
    wide[...] = incoming_ref[...].astype(jnp.float32)
    for r in range(capacity):
        for c in range(chunks):
            received[r * peers : (r + 1) * peers, c * LANES : (c + 1) * LANES] = wide[
                pl.ds(r * chunks + c, peers, stride=stride), :
            ].astype(jnp.bfloat16)
    labels = wide[pl.ds(capacity * chunks, peers, stride=stride), :]
    group = group_ref[...].astype(jnp.float32) + 1.0
    for r in range(capacity):
        bias[r * peers : (r + 1) * peers, :] = jnp.where(labels[:, r : r + 1] == group, 0.0, FAR)

    def columns_of(head):
        return slice(head * HEAD_DIM, (head + 1) * HEAD_DIM)

    def products(head):
        at, of_values = columns_of(head), columns_of(HEADS + head)
        score = contract(received[:, at], query_ref[:, at], ((1,), (1,))) * scale + bias[...]
        value_dot = contract(received[:, of_values], grad_ref[:, at], ((1,), (1,)))
        return score, value_dot

    def softmax(score, value_dot):
        top = jnp.maximum(jnp.max(score, axis=0, keepdims=True), 0.0)
        expo = jnp.exp(score - top)
        weight = expo * (1.0 / (jnp.exp(-top) + jnp.sum(expo, axis=0, keepdims=True)))
        probs = weight.astype(jnp.bfloat16)
        delta = jnp.sum(probs.astype(jnp.float32) * value_dot, axis=0, keepdims=True)
        return probs, (weight * ((value_dot - delta) * scale)).astype(jnp.bfloat16)

    def gradients(head, probs, score_grad):
        at = columns_of(head)
        key_grad = contract(score_grad, query_ref[:, at], ((1,), (0,)))
        value_grad = contract(probs, grad_ref[:, at], ((1,), (0,)))
        query_grad_ref[:, at] = contract(score_grad, received[:, at], ((0,), (0,))).astype(jnp.bfloat16)
        for r in range(capacity):
            rows = slice(r * peers, (r + 1) * peers)
            for c, part in ((head, key_grad), (HEADS + head, value_grad)):
                wide[pl.ds(r * chunks + c, peers, stride=capacity * chunks), :] = part[rows]

    scores, weights = {}, {}
    for turn in range(HEADS + 2):
        if turn < HEADS:
            scores[turn] = products(turn)
        if 0 <= turn - 1 < HEADS:
            weights[turn - 1] = softmax(*scores.pop(turn - 1))
        if turn >= 2:
            gradients(turn - 2, *weights.pop(turn - 2))
    out_ref[...] = wide[: slot_count * chunks, :].astype(jnp.bfloat16)


def columns_kernel(returned_ref, placing_ref, out_ref, wide):
    wide[...] = returned_ref[...].astype(jnp.float32)
    slot_count = placing_ref.shape[1]
    chunks = returned_ref.shape[0] // slot_count
    for c in range(chunks):
        rows = wide[pl.ds(c, slot_count, stride=chunks), :].astype(jnp.bfloat16)
        turned_rows = contract(rows, placing_ref[...], ((0,), (1,)))
        out_ref[c * LANES : (c + 1) * LANES, :] = turned_rows.astype(jnp.bfloat16)
    extra = out_ref.shape[0] - chunks * LANES
    if extra:
        out_ref[chunks * LANES :, :] = jnp.zeros((extra, out_ref.shape[1]), jnp.bfloat16)


def tile_kernel(
    block, share, norm_factor, order_ref, blocks_ref, own_hbm, other_hbm, out_ref, rows, near, total, sems
):
    multiply = product(rows, [own_hbm, other_hbm], near, sems, total)
    groups, enc_rows = blocks_ref.shape[0], blocks_ref.shape[2]
    for k in range(groups):
        rows[:, k * enc_rows : (k + 1) * enc_rows] = blocks_ref[order_ref[k]]
    multiply()
    kept = out_ref.shape[1]
    low = lax.broadcasted_iota(jnp.int32, (kept, LANES), 1) < share
    for p in range(total.shape[1] // LANES):
        two = total[:, p * LANES : (p + 1) * LANES] * norm_factor
        first, second = two[:kept], two[block - kept :]
        out_ref[2 * p] = jnp.where(low, first, pltpu.roll(second, share, 1)).astype(jnp.bfloat16)
        out_ref[2 * p + 1] = jnp.where(low, pltpu.roll(first, share, 1), second).astype(jnp.bfloat16)


def sum_kernel(block, share, parts_ref, out_ref):
    kept = parts_ref.shape[1]
    total = parts_ref[0].astype(jnp.float32)
    for i in range(1, parts_ref.shape[0]):
        total += parts_ref[i].astype(jnp.float32)
    columns = total.T
    out_ref[:, :kept] = columns[:share].astype(jnp.bfloat16)
    out_ref[:, kept:] = columns[share:, 2 * kept - block :].astype(jnp.bfloat16)


def final_kernel(block, totals_ref, out_ref):
    for g in range(totals_ref.shape[1]):
        total = totals_ref[0, g].astype(jnp.float32)
        for t in range(1, totals_ref.shape[0]):
            total += totals_ref[t, g].astype(jnp.float32)
        out_ref[:, g * block : (g + 1) * block] = total


def shards(enc, enc_dest, enc_group, query, dec_group, out_grad, w_kv):
    peers = lax.axis_size("seq")
    parts = lax.axis_size("part")
    line = lax.axis_size("line")
    groups = line * lax.axis_size("core")
    enc_rows, model = enc.shape
    capacity = 3 * enc_rows // (2 * peers)
    slot_count = peers * capacity
    full = w_kv.shape[1]
    width = full // 2
    dec_rows = query.shape[0]
    norm_factor = 1.0 / math.sqrt(enc_rows * peers * groups * parts)
    block = -(-full // (groups * 8)) * 8
    kept = -(-block // 32) * 16
    share = model // peers
    chunks = full // LANES
    packed_rows = capacity * chunks
    stride = packed_rows + 8

    outgoing, placing = pl.pallas_call(
        functools.partial(route_kernel, peers, capacity, stride),
        out_shape=(
            jax.ShapeDtypeStruct((peers * stride, LANES), jnp.bfloat16),
            jax.ShapeDtypeStruct((enc_rows, slot_count), jnp.bfloat16),
        ),
        in_specs=[pl.BlockSpec(memory_space=pltpu.HBM)] * 4,
        scratch_shapes=[
            pltpu.VMEM((enc_rows, model), jnp.bfloat16),
            pltpu.VMEM((2, 1, enc_rows), jnp.int32),
            pltpu.VMEM((model, full), jnp.bfloat16),
            pltpu.VMEM((enc_rows, full), jnp.float32),
            pltpu.VMEM((peers * stride, LANES), jnp.float32),
            pltpu.SemaphoreType.DMA((3,)),
            pltpu.SemaphoreType.DMA((4,)),
        ],
        compiler_params=pltpu.CompilerParams(vmem_limit_bytes=64 * MIB),
    )(enc, enc_dest.reshape(1, enc_rows), enc_group.reshape(1, enc_rows), w_kv)
    mine, outgoing = lax.optimization_barrier((enc, outgoing))
    passed = [lax.ppermute(mine, "line", [(i, i ^ k) for i in range(line)]) for k in range(line - 1, 0, -1)]
    incoming = lax.all_to_all(
        outgoing.reshape(peers, stride, LANES), "seq", split_axis=0, concat_axis=0, tiled=True
    )

    query_near, grad_near, group_near, placing_near = stage(
        (query, out_grad, dec_group.reshape(1, dec_rows), placing), placing
    )
    query_grad, slot_grad = pl.pallas_call(
        functools.partial(attention_kernel, peers, capacity, stride),
        out_shape=(
            jax.ShapeDtypeStruct((dec_rows, width), jnp.bfloat16),
            jax.ShapeDtypeStruct((peers * packed_rows, LANES), jnp.bfloat16),
        ),
        scratch_shapes=[
            pltpu.VMEM((peers * stride, LANES), jnp.float32),
            pltpu.VMEM((slot_count, full), jnp.bfloat16),
            pltpu.VMEM((slot_count, dec_rows), jnp.float32),
        ],
        compiler_params=pltpu.CompilerParams(vmem_limit_bytes=32 * MIB),
    )(incoming.reshape(peers * stride, LANES), group_near, query_near, grad_near)
    *passed, _ = lax.optimization_barrier((*passed, slot_grad))
    own = jnp.concatenate([enc] + passed[::-1])
    other = lax.ppermute(own, "core", [(0, 1), (1, 0)])
    returned = lax.all_to_all(
        slot_grad.reshape(peers, packed_rows, LANES), "seq", split_axis=0, concat_axis=0, tiled=True
    )

    columns = pl.pallas_call(
        columns_kernel,
        out_shape=jax.ShapeDtypeStruct((groups * block, enc_rows), jnp.bfloat16),
        scratch_shapes=[pltpu.VMEM((peers * packed_rows, LANES), jnp.float32)],
        compiler_params=pltpu.CompilerParams(vmem_limit_bytes=32 * MIB),
    )(returned.reshape(peers * packed_rows, LANES), placing_near)
    enc_grad = contract(columns[:full], w_kv, ((0,), (1,))).astype(jnp.bfloat16)

    blocks = lax.all_to_all(
        columns.reshape(groups, block, enc_rows), ("line", "core"), split_axis=0, concat_axis=0, tiled=True
    )
    place = jnp.arange(groups, dtype=jnp.int32)
    order = (lax.axis_index("line") ^ place % line) * 2 + (lax.axis_index("core") ^ place // line)
    tile = pl.pallas_call(
        functools.partial(tile_kernel, block, share, norm_factor),
        out_shape=jax.ShapeDtypeStruct((peers, kept, 2 * share), jnp.bfloat16),
        in_specs=[
            pl.BlockSpec(memory_space=pltpu.SMEM),
            pl.BlockSpec(memory_space=pltpu.VMEM),
            pl.BlockSpec(memory_space=pltpu.HBM),
            pl.BlockSpec(memory_space=pltpu.HBM),
        ],
        scratch_shapes=[
            pltpu.VMEM((block, groups * enc_rows), jnp.bfloat16),
            pltpu.VMEM((groups * enc_rows, model), jnp.bfloat16),
            pltpu.VMEM((block, model), jnp.float32),
            pltpu.SemaphoreType.DMA((groups // 2,)),
        ],
        compiler_params=pltpu.CompilerParams(vmem_limit_bytes=32 * MIB),
    )(order, blocks, own, other)
    tiles = lax.all_to_all(tile, "seq", split_axis=0, concat_axis=0, tiled=True)
    shared = pl.pallas_call(
        functools.partial(sum_kernel, block, share),
        out_shape=jax.ShapeDtypeStruct((share, block), jnp.bfloat16),
        compiler_params=pltpu.CompilerParams(vmem_limit_bytes=32 * MIB),
    )(tiles)
    totals = lax.all_gather(shared, ("part", "line", "core"), axis=0, tiled=True)
    kv_weight_grad = pl.pallas_call(
        functools.partial(final_kernel, block),
        out_shape=jax.ShapeDtypeStruct((share, full), jnp.float32),
        compiler_params=pltpu.CompilerParams(vmem_limit_bytes=32 * MIB),
    )(totals.reshape(parts, groups, share, block))
    return (query_grad, enc_grad, kv_weight_grad)


def solution(mesh):
    dp, seq = mesh.devices.shape
    names = ("part", "line", "core", "seq")
    cut = Mesh(mesh.devices.reshape(dp // (2 * LINE), LINE, 2, seq), names)
    in_specs = (P(names, None), P(names, None), P(names), P(names, None), P(names), P(names, None), P())
    out_specs = (P(names, None), P(names, None), P("seq", None))
    return jax.shard_map(shards, mesh=cut, in_specs=in_specs, out_specs=out_specs, check_vma=False)
```

```python
import functools
import math

import jax
import jax.numpy as jnp
from jax import lax
from jax.experimental import pallas as pl
from jax.experimental.pallas import tpu as pltpu
from jax.sharding import Mesh, PartitionSpec as P

HEADS = 8
HEAD_DIM = 128
LANES = 128
FAR = -1e30
MIB = 1 << 20
LINE = 4


def contract(a, b, dims):
    return lax.dot_general(a, b, (dims, ((), ())), preferred_element_type=jnp.float32)


def product(rows, sources, near, sems, total):
    count = sems.shape[0]
    depth = near.shape[0] // count
    each = count // len(sources)
    spans = [pl.ds(k * depth, depth) for k in range(count)]
    copies = [
        pltpu.make_async_copy(sources[k // each].at[spans[k % each]], near.at[spans[k]], sems.at[k])
        for k in range(count)
    ]
    for copy in copies:
        copy.start()

    def run():
        for k in range(count):
            copies[k].wait()
            at = slice(k * depth, (k + 1) * depth)
            part = contract(rows[:, at], near[at, :], ((1,), (0,)))
            total[...] = part if k == 0 else total[...] + part

    return run


def turned(row, diagonal):
    return jnp.sum(jnp.where(diagonal, row.astype(jnp.float32), 0.0), axis=1, keepdims=True)


def route_kernel(
    peers,
    capacity,
    stride,
    enc_hbm,
    dest_hbm,
    group_hbm,
    w_hbm,
    out_ref,
    placing_ref,
    enc_ref,
    row_refs,
    w_ref,
    kv,
    wide,
    sems,
    w_sems,
):
    copies = [
        pltpu.make_async_copy(dest_hbm, row_refs.at[0], sems.at[0]),
        pltpu.make_async_copy(group_hbm, row_refs.at[1], sems.at[1]),
        pltpu.make_async_copy(enc_hbm, enc_ref, sems.at[2]),
    ]
    for copy in copies:
        copy.start()
    multiply = product(enc_ref, [w_hbm], w_ref, w_sems, kv)
    rows = enc_ref.shape[0]
    chunks = kv.shape[1] // LANES
    ahead = lax.broadcasted_iota(jnp.int32, (rows, rows), 0)
    behind = lax.broadcasted_iota(jnp.int32, (rows, rows), 1)
    earlier = jnp.where(behind < ahead, 1.0, 0.0).astype(jnp.bfloat16)
    copies[0].wait()
    copies[1].wait()
    dest = turned(row_refs[0], ahead == behind).astype(jnp.int32)
    label = turned(row_refs[1] + 1, ahead == behind)
    owner = lax.broadcasted_iota(jnp.int32, (rows, peers), 1)
    hits = jnp.where(owner == dest, 1.0, 0.0)
    before = contract(earlier, hits.astype(jnp.bfloat16), ((1,), (0,)))
    rank = jnp.sum(before * hits, axis=1, keepdims=True).astype(jnp.int32)
    slot = lax.broadcasted_iota(jnp.int32, (rows, peers * capacity), 1)
    placing_ref[...] = jnp.where(slot == dest * capacity + rank, 1.0, 0.0).astype(jnp.bfloat16)
    placing = jnp.where(slot == rank * peers + dest, 1.0, 0.0).astype(jnp.bfloat16)
    lane = lax.broadcasted_iota(jnp.int32, (rows, LANES), 1)
    spots = jnp.where(lane == rank, label, 0.0).astype(jnp.bfloat16)
    labels = contract(hits.astype(jnp.bfloat16), spots, ((0,), (0,)))
    for extra in range(capacity * chunks, stride):
        wide[pl.ds(extra, peers, stride=stride), :] = labels
    copies[2].wait()
    multiply()
    slots = contract(placing, kv[...].astype(jnp.bfloat16), ((0,), (0,)))
    for r in range(capacity):
        for c in range(chunks):
            wide[pl.ds(r * chunks + c, peers, stride=stride), :] = slots[
                r * peers : (r + 1) * peers, c * LANES : (c + 1) * LANES
            ]
    out_ref[...] = wide[...].astype(jnp.bfloat16)


def stage_kernel(count, *refs):
    sources, targets, sems = refs[:count], refs[-count - 1 : -1], refs[-1]
    copies = [
        pltpu.make_async_copy(source, target, sems.at[k])
        for k, (source, target) in enumerate(zip(sources, targets))
    ]
    for copy in copies:
        copy.start()
    for copy in copies:
        copy.wait()


def stage(arrays, after):
    count = len(arrays)
    return pl.pallas_call(
        functools.partial(stage_kernel, count),
        out_shape=tuple(jax.ShapeDtypeStruct(a.shape, a.dtype) for a in arrays),
        in_specs=[pl.BlockSpec(memory_space=pltpu.HBM)] * count + [pl.BlockSpec(memory_space=pl.ANY)],
        out_specs=tuple(pl.BlockSpec(memory_space=pltpu.VMEM) for a in arrays),
        scratch_shapes=[pltpu.SemaphoreType.DMA((count,))],
        compiler_params=pltpu.CompilerParams(vmem_limit_bytes=32 * MIB),
    )(*arrays, after)


def attention_kernel(
    peers,
    capacity,
    stride,
    incoming_ref,
    group_ref,
    query_ref,
    grad_ref,
    query_grad_ref,
    out_ref,
    wide,
    received,
    bias,
):
    slot_count, model = received.shape
    chunks = model // LANES
    width = HEADS * HEAD_DIM
    scale = 1.0 / math.sqrt(HEAD_DIM)
    wide[...] = incoming_ref[...].astype(jnp.float32)
    for r in range(capacity):
        for c in range(chunks):
            received[r * peers : (r + 1) * peers, c * LANES : (c + 1) * LANES] = wide[
                pl.ds(r * chunks + c, peers, stride=stride), :
            ].astype(jnp.bfloat16)
    labels = wide[pl.ds(capacity * chunks, peers, stride=stride), :]
    group = group_ref[...].astype(jnp.float32) + 1.0
    for r in range(capacity):
        bias[r * peers : (r + 1) * peers, :] = jnp.where(labels[:, r : r + 1] == group, 0.0, FAR)

    def columns_of(head):
        return slice(head * HEAD_DIM, (head + 1) * HEAD_DIM)

    def products(head):
        at, of_values = columns_of(head), columns_of(HEADS + head)
        score = contract(received[:, at], query_ref[:, at], ((1,), (1,))) * scale + bias[...]
        value_dot = contract(received[:, of_values], grad_ref[:, at], ((1,), (1,)))
        return score, value_dot

    def softmax(score, value_dot):
        top = jnp.maximum(jnp.max(score, axis=0, keepdims=True), 0.0)
        expo = jnp.exp(score - top)
        weight = expo * (1.0 / (jnp.exp(-top) + jnp.sum(expo, axis=0, keepdims=True)))
        probs = weight.astype(jnp.bfloat16)
        delta = jnp.sum(probs.astype(jnp.float32) * value_dot, axis=0, keepdims=True)
        return probs, (weight * ((value_dot - delta) * scale)).astype(jnp.bfloat16)

    def gradients(head, probs, score_grad):
        at = columns_of(head)
        key_grad = contract(score_grad, query_ref[:, at], ((1,), (0,)))
        value_grad = contract(probs, grad_ref[:, at], ((1,), (0,)))
        query_grad_ref[:, at] = contract(score_grad, received[:, at], ((0,), (0,))).astype(jnp.bfloat16)
        for r in range(capacity):
            rows = slice(r * peers, (r + 1) * peers)
            for c, part in ((head, key_grad), (HEADS + head, value_grad)):
                wide[pl.ds(r * chunks + c, peers, stride=capacity * chunks), :] = part[rows]

    scores, weights = {}, {}
    for turn in range(HEADS + 2):
        if turn < HEADS:
            scores[turn] = products(turn)
        if 0 <= turn - 1 < HEADS:
            weights[turn - 1] = softmax(*scores.pop(turn - 1))
        if turn >= 2:
            gradients(turn - 2, *weights.pop(turn - 2))
    out_ref[...] = wide[: slot_count * chunks, :].astype(jnp.bfloat16)


def columns_kernel(returned_ref, placing_ref, out_ref, wide):
    wide[...] = returned_ref[...].astype(jnp.float32)
    slot_count = placing_ref.shape[1]
    chunks = returned_ref.shape[0] // slot_count
    for c in range(chunks):
        rows = wide[pl.ds(c, slot_count, stride=chunks), :].astype(jnp.bfloat16)
        turned_rows = contract(rows, placing_ref[...], ((0,), (1,)))
        out_ref[c * LANES : (c + 1) * LANES, :] = turned_rows.astype(jnp.bfloat16)
    extra = out_ref.shape[0] - chunks * LANES
    if extra:
        out_ref[chunks * LANES :, :] = jnp.zeros((extra, out_ref.shape[1]), jnp.bfloat16)


def tile_kernel(
    block, share, norm_factor, order_ref, blocks_ref, own_hbm, other_hbm, out_ref, rows, near, total, sems
):
    multiply = product(rows, [own_hbm, other_hbm], near, sems, total)
    groups, enc_rows = blocks_ref.shape[0], blocks_ref.shape[2]
    for k in range(groups):
        rows[:, k * enc_rows : (k + 1) * enc_rows] = blocks_ref[order_ref[k]]
    multiply()
    kept = out_ref.shape[1]
    low = lax.broadcasted_iota(jnp.int32, (kept, LANES), 1) < share
    for p in range(total.shape[1] // LANES):
        two = total[:, p * LANES : (p + 1) * LANES] * norm_factor
        first, second = two[:kept], two[block - kept :]
        out_ref[2 * p] = jnp.where(low, first, pltpu.roll(second, share, 1)).astype(jnp.bfloat16)
        out_ref[2 * p + 1] = jnp.where(low, pltpu.roll(first, share, 1), second).astype(jnp.bfloat16)


def sum_kernel(block, share, parts_ref, out_ref):
    kept = parts_ref.shape[1]
    total = parts_ref[0].astype(jnp.float32)
    for i in range(1, parts_ref.shape[0]):
        total += parts_ref[i].astype(jnp.float32)
    columns = total.T
    out_ref[:, :kept] = columns[:share].astype(jnp.bfloat16)
    out_ref[:, kept:] = columns[share:, 2 * kept - block :].astype(jnp.bfloat16)


def final_kernel(block, totals_ref, out_ref):
    for g in range(totals_ref.shape[1]):
        total = totals_ref[0, g].astype(jnp.float32)
        for t in range(1, totals_ref.shape[0]):
            total += totals_ref[t, g].astype(jnp.float32)
        out_ref[:, g * block : (g + 1) * block] = total


def shards(enc, enc_dest, enc_group, query, dec_group, out_grad, w_kv):
    peers = lax.axis_size("seq")
    parts = lax.axis_size("part")
    line = lax.axis_size("line")
    groups = line * lax.axis_size("core")
    enc_rows, model = enc.shape
    capacity = 3 * enc_rows // (2 * peers)
    slot_count = peers * capacity
    full = w_kv.shape[1]
    width = full // 2
    dec_rows = query.shape[0]
    norm_factor = 1.0 / math.sqrt(enc_rows * peers * groups * parts)
    block = -(-full // (groups * 8)) * 8
    kept = -(-block // 32) * 16
    share = model // peers
    chunks = full // LANES
    packed_rows = capacity * chunks
    stride = packed_rows + 8

    outgoing, placing = pl.pallas_call(
        functools.partial(route_kernel, peers, capacity, stride),
        out_shape=(
            jax.ShapeDtypeStruct((peers * stride, LANES), jnp.bfloat16),
            jax.ShapeDtypeStruct((enc_rows, slot_count), jnp.bfloat16),
        ),
        in_specs=[pl.BlockSpec(memory_space=pltpu.HBM)] * 4,
        scratch_shapes=[
            pltpu.VMEM((enc_rows, model), jnp.bfloat16),
            pltpu.VMEM((2, 1, enc_rows), jnp.int32),
            pltpu.VMEM((model, full), jnp.bfloat16),
            pltpu.VMEM((enc_rows, full), jnp.float32),
            pltpu.VMEM((peers * stride, LANES), jnp.float32),
            pltpu.SemaphoreType.DMA((3,)),
            pltpu.SemaphoreType.DMA((4,)),
        ],
        compiler_params=pltpu.CompilerParams(vmem_limit_bytes=64 * MIB),
    )(enc, enc_dest.reshape(1, enc_rows), enc_group.reshape(1, enc_rows), w_kv)
    mine, outgoing = lax.optimization_barrier((enc, outgoing))
    passed = [lax.ppermute(mine, "line", [(i, i ^ k) for i in range(line)]) for k in range(line - 1, 0, -1)]
    incoming = lax.all_to_all(
        outgoing.reshape(peers, stride, LANES), "seq", split_axis=0, concat_axis=0, tiled=True
    )

    query_near, grad_near, group_near, placing_near = stage(
        (query, out_grad, dec_group.reshape(1, dec_rows), placing), placing
    )
    query_grad, slot_grad = pl.pallas_call(
        functools.partial(attention_kernel, peers, capacity, stride),
        out_shape=(
            jax.ShapeDtypeStruct((dec_rows, width), jnp.bfloat16),
            jax.ShapeDtypeStruct((peers * packed_rows, LANES), jnp.bfloat16),
        ),
        scratch_shapes=[
            pltpu.VMEM((peers * stride, LANES), jnp.float32),
            pltpu.VMEM((slot_count, full), jnp.bfloat16),
            pltpu.VMEM((slot_count, dec_rows), jnp.float32),
        ],
        compiler_params=pltpu.CompilerParams(vmem_limit_bytes=32 * MIB),
    )(incoming.reshape(peers * stride, LANES), group_near, query_near, grad_near)
    *passed, _ = lax.optimization_barrier((*passed, slot_grad))
    own = jnp.concatenate([enc] + passed[::-1])
    other = lax.ppermute(own, "core", [(0, 1), (1, 0)])
    returned = lax.all_to_all(
        slot_grad.reshape(peers, packed_rows, LANES), "seq", split_axis=0, concat_axis=0, tiled=True
    )

    columns = pl.pallas_call(
        columns_kernel,
        out_shape=jax.ShapeDtypeStruct((groups * block, enc_rows), jnp.bfloat16),
        scratch_shapes=[pltpu.VMEM((peers * packed_rows, LANES), jnp.float32)],
        compiler_params=pltpu.CompilerParams(vmem_limit_bytes=32 * MIB),
    )(returned.reshape(peers * packed_rows, LANES), placing_near)
    enc_grad = contract(columns[:full], w_kv, ((0,), (1,))).astype(jnp.bfloat16)

    blocks = lax.all_to_all(
        columns.reshape(groups, block, enc_rows), ("line", "core"), split_axis=0, concat_axis=0, tiled=True
    )
    blocks, enc_grad = lax.optimization_barrier((blocks, enc_grad))
    place = jnp.arange(groups, dtype=jnp.int32)
    order = (lax.axis_index("line") ^ place % line) * 2 + (lax.axis_index("core") ^ place // line)
    tile = pl.pallas_call(
        functools.partial(tile_kernel, block, share, norm_factor),
        out_shape=jax.ShapeDtypeStruct((peers, kept, 2 * share), jnp.bfloat16),
        in_specs=[
            pl.BlockSpec(memory_space=pltpu.SMEM),
            pl.BlockSpec(memory_space=pltpu.VMEM),
            pl.BlockSpec(memory_space=pltpu.HBM),
            pl.BlockSpec(memory_space=pltpu.HBM),
        ],
        scratch_shapes=[
            pltpu.VMEM((block, groups * enc_rows), jnp.bfloat16),
            pltpu.VMEM((groups * enc_rows, model), jnp.bfloat16),
            pltpu.VMEM((block, model), jnp.float32),
            pltpu.SemaphoreType.DMA((groups // 2,)),
        ],
        compiler_params=pltpu.CompilerParams(vmem_limit_bytes=32 * MIB),
    )(order, blocks, own, other)
    tiles = lax.all_to_all(tile, "seq", split_axis=0, concat_axis=0, tiled=True)
    shared = pl.pallas_call(
        functools.partial(sum_kernel, block, share),
        out_shape=jax.ShapeDtypeStruct((share, block), jnp.bfloat16),
        compiler_params=pltpu.CompilerParams(vmem_limit_bytes=32 * MIB),
    )(tiles)
    totals = lax.all_gather(shared, ("part", "line", "core"), axis=0, tiled=True)
    kv_weight_grad = pl.pallas_call(
        functools.partial(final_kernel, block),
        out_shape=jax.ShapeDtypeStruct((share, full), jnp.float32),
        compiler_params=pltpu.CompilerParams(vmem_limit_bytes=32 * MIB),
    )(totals.reshape(parts, groups, share, block))
    return (query_grad, enc_grad, kv_weight_grad)


def solution(mesh):
    dp, seq = mesh.devices.shape
    names = ("part", "line", "core", "seq")
    cut = Mesh(mesh.devices.reshape(dp // (2 * LINE), LINE, 2, seq), names)
    in_specs = (P(names, None), P(names, None), P(names), P(names, None), P(names), P(names, None), P())
    out_specs = (P(names, None), P(names, None), P("seq", None))
    return jax.shard_map(shards, mesh=cut, in_specs=in_specs, out_specs=out_specs, check_vma=False)
```
